128 devices in a mesh: row: 8 (over x_hi, z), col: 16 (over y, x_lo, core).
Axes of the slice: x: 4 (x_hi: 2, x_lo: 2; x = x_hi * 2 + x_lo), y: 4, z: 4, core: 2. Of those that a mesh axis runs over, the one named last changes fastest.
Arguments:
- features: bfloat16 [65536, 512], P(('row', 'col')), may hold values from -6 to 6
- weight: bfloat16 [512, 512], replicated, may hold values from -0.25 to 0.25
- bias: float32 [512], replicated, may hold values from -3 to 3
- cotangent: bfloat16 [65536, 512], P(('row', 'col')), may hold values from -6 to 6
- tile_values: bfloat16 [49152, 128, 128], P(('row', 'col')), may hold values from -0.09375 to 0.09375
- tile_row: int32 [128, 384], P(('row', 'col')), may hold values from 0 to 63
- tile_col: int32 [128, 384], P(('row', 'col')), may hold values from 0 to 31
- tile_count: int32 [128], P(('row', 'col')), may hold values from 48 to 384, as said below
Outputs:
- output: bfloat16 [65536, 512], P(('row', 'col'))
- grad_features: bfloat16 [65536, 512], P(('row', 'col'))
- grad_weight: float32 [512, 512], replicated
- grad_bias: float32 [512], replicated
The draws below stay inside these ranges and needn't reach their ends.
Inputs may be any that keep to these rules, and one draw needn't show every extreme that they name: Each device uses slots 0 to tile_count - 1 of its lists; some device uses all 384 slots. `tile_row`: A tile position may be listed more than once; such tiles add.
All inputs are finite; a program needn't handle non-finite values.
Results may differ from the reference program's by a relative error of at most 0.024.
Values may be sent and summed in bfloat16 or wider, within the bound.
No kernel may reach another device: no remote copies, remote signals or barrier semaphores. Data moves between devices by JAX's collectives and lax.ppermute only.
A program may use at most 192 MiB of HBM per device.

```python
import jax
import jax.numpy as jnp
from jax import lax

FEAT = 512
TILE = 128
NODE_DEV = 512
TILES_DEV = 384
GRID = 128
NODES = 65536
RB = 64
CB = 32
N_ROW = 8
N_COL = 16


def draw_tile_count(key, part):
    key = jax.random.fold_in(key, 7)
    key_one, key_two, key_three = jax.random.split(key, 3)
    lowest = max(1, TILES_DEV // 8)
    draw_one = jax.random.randint(key_one, (GRID,), lowest, TILES_DEV + 1)
    draw_two = jax.random.randint(key_two, (GRID,), lowest, TILES_DEV + 1)
    counts = jnp.minimum(draw_one, draw_two)
    busiest = jax.random.randint(key_three, (), 0, GRID)
    return counts.at[busiest].set(TILES_DEV).astype(jnp.int32)


def with_ends(result, rng, least, top_value):
    spot = [jax.random.randint(jax.random.fold_in(rng, axis), (), 0, length) for axis, length in enumerate(result.shape)]
    widest = result.shape.index(max(result.shape))
    next_to = spot[:widest] + [(spot[widest] + 1) % result.shape[widest]] + spot[widest + 1:]
    return result.at[tuple(spot)].set(least).at[tuple(next_to)].set(top_value)


def steps_of(own_key, dims, cuts, least, high):
    loudness = 1.0
    for position, parts in cuts:
        draws = jax.random.uniform(jax.random.fold_in(jax.random.fold_in(own_key, 6), position), (parts,), jnp.float32, least / len(cuts), high / len(cuts))
        loudness = loudness * jnp.repeat(jnp.exp(draws), dims[position] // parts).reshape((-1,) + (1,) * (len(dims) - 1 - position))
    return loudness


def centred(rng, shape, deviation, reach, cuts=(), held_as=jnp.bfloat16):
    gain = steps_of(rng, shape, cuts, -0.22, 0.18) if cuts else 1.0
    entries = jax.random.normal(rng, shape, jnp.float32) * deviation * gain
    return jnp.minimum(jnp.maximum(entries, -reach), reach).astype(held_as)


def setup_inputs(seed: int = 0) -> dict:
    splits = jax.random.split(jax.random.key(seed), 9)
    features = centred(splits[0], (NODES, FEAT), 1.0, 6.0, ((0, 128),))
    weight = centred(splits[1], (FEAT, FEAT), FEAT ** -0.5, 0.25)
    bias = centred(splits[2], (FEAT,), 0.5, 3.0, (), jnp.float32)
    cotangent = centred(splits[3], (NODES, FEAT), 1.0, 6.0, ((0, 128),))
    tile_values = centred(splits[4], (GRID * TILES_DEV, TILE, TILE), (TILES_DEV * 6400 // NODE_DEV) ** -0.5, 0.09375, ((0, 128),))
    tile_row = with_ends(jax.random.randint(splits[5], (GRID, TILES_DEV), 0, RB), jax.random.fold_in(splits[5], 1), 0, RB - 1).astype(jnp.int32)
    tile_col = with_ends(jax.random.randint(splits[6], (GRID, TILES_DEV), 0, CB), jax.random.fold_in(splits[6], 1), 0, CB - 1).astype(jnp.int32)
    tile_count = draw_tile_count(jax.random.fold_in(splits[8], 71), 0)
    return {"features": features, "weight": weight, "bias": bias, "cotangent": cotangent, "tile_values": tile_values, "tile_row": tile_row, "tile_col": tile_col, "tile_count": tile_count}


def tile_product(values, block_rows, block_columns, in_use, source, out_rows, transpose):
    width = source.shape[1]
    blocks = source.reshape(-1, TILE, width).astype(jnp.float32)
    if transpose:
        picked = blocks[block_rows]
        target = block_columns
        form = "tji,tjf->tif"
    else:
        picked = blocks[block_columns]
        target = block_rows
        form = "tij,tjf->tif"
    product = jnp.einsum(form, values.astype(jnp.float32), picked, precision=lax.Precision.HIGHEST)
    product = product * in_use[:, None, None]
    totals = jnp.zeros((out_rows // TILE, TILE, width), jnp.float32).at[target].add(product)
    return totals.reshape(out_rows, width)


def round_trip(array):
    return lax.optimization_barrier(array.astype(jnp.bfloat16)).astype(jnp.float32)


def reference(features, weight, bias, cotangent, tile_values, tile_row, tile_col, tile_count):
    width = features.shape[1]
    hidden = jnp.dot(features, weight, preferred_element_type=jnp.float32).astype(jnp.bfloat16)
    values = tile_values.reshape(GRID, TILES_DEV, TILE, TILE)
    in_use = (jnp.arange(TILES_DEV, dtype=jnp.int32)[None, :] < tile_count[:, None]).astype(jnp.float32)
    grouped = hidden.reshape(N_ROW, N_COL, NODE_DEV, width)
    row_parts = []
    for row_index in range(N_ROW):
        def advance(totals, column_index):
            device = row_index * N_COL + column_index
            source = lax.dynamic_index_in_dim(grouped, column_index, 1, keepdims=False).reshape(-1, width)
            part = tile_product(values[device], tile_row[device], tile_col[device], in_use[device], source, RB * TILE, False)
            return totals + round_trip(part), None
        totals, unused = lax.scan(advance, jnp.zeros((RB * TILE, width), jnp.float32), jnp.arange(N_COL, dtype=jnp.int32))
        row_parts.append(totals)
    summed_input = jnp.concatenate(row_parts, axis=0) + bias.astype(jnp.float32)[None, :]
    sigma = jax.nn.sigmoid(summed_input)
    output = (summed_input * sigma).astype(jnp.bfloat16)
    grad_pre = (cotangent.astype(jnp.float32) * sigma * (1.0 + summed_input * (1.0 - sigma))).astype(jnp.bfloat16)
    grad_bias = jnp.sum(grad_pre.astype(jnp.float32), axis=0)
    column_parts = []
    for column_index in range(N_COL):
        def advance_back(totals, row_index):
            device = row_index * N_COL + column_index
            source = lax.dynamic_slice_in_dim(grad_pre, (row_index * (RB * TILE)).astype(jnp.int32), RB * TILE, 0)
            part = tile_product(values[device], tile_row[device], tile_col[device], in_use[device], source, CB * TILE, True)
            return totals + round_trip(part), None
        totals, unused = lax.scan(advance_back, jnp.zeros((CB * TILE, width), jnp.float32), jnp.arange(N_ROW, dtype=jnp.int32))
        column_parts.append(totals)
    back_sum = jnp.stack(column_parts, axis=0).reshape(N_COL, N_ROW, NODE_DEV, width)
    back_sum = back_sum.transpose(1, 0, 2, 3).reshape(NODES, width)
    grad_features = jnp.dot(back_sum.astype(jnp.bfloat16), weight.T, preferred_element_type=jnp.float32).astype(jnp.bfloat16)
    grad_weight = jnp.dot(features.astype(jnp.float32).T, back_sum, precision=lax.Precision.HIGHEST)
    return (output, grad_features, grad_weight, grad_bias)
```

```python
import functools

import jax
import jax.numpy as jnp
from jax import lax
from jax.experimental import pallas as pl
from jax.experimental.pallas import tpu as pltpu
from jax.sharding import PartitionSpec as P

CHUNKS = 1
GROUP = 16
TILE = 128
SPAN = 512
BF = jnp.bfloat16
F32 = jnp.float32


def product_kernel(n_src, n_out, transpose, count_ref, src_idx, dst_idx, values, *refs):
    sources, outs = refs[:n_src], refs[n_src : n_src + n_out]
    source, total = refs[n_src + n_out :]
    step = pl.program_id(0)

    @pl.when(step == 0)
    def _():
        at = 0
        for ref in sources:
            source[at : at + ref.shape[0], :] = ref[...]
            at += ref.shape[0]
        total[...] = jnp.zeros_like(total)

    def one(t):
        slot = step * GROUP + t
        start = pl.multiple_of(src_idx[slot] * TILE, TILE)
        end = pl.multiple_of(dst_idx[slot] * TILE, TILE)
        block = source[pl.ds(start, TILE), :]
        dims = (((0,), (0,)), ((), ())) if transpose else (((1,), (0,)), ((), ()))
        total[pl.ds(end, TILE), :] += lax.dot_general(
            values[t], block, dims, preferred_element_type=F32
        )

    left = count_ref[0] - step * GROUP

    @pl.when(left >= GROUP)
    def _():
        for t in range(GROUP):
            one(t)

    @pl.when((left > 0) & (left < GROUP))
    def _():
        @pl.loop(0, left)
        def _(t):
            one(t)

    @pl.when(step == pl.num_programs(0) - 1)
    def _():
        at = 0
        for ref in outs:
            ref[...] = total[at : at + ref.shape[0], :].astype(BF)
            at += ref.shape[0]


def product(values, count, src_idx, dst_idx, sources, chunk, width, out_rows, transpose):
    rows = sum(s.shape[0] for s in sources)

    def tile_at(i, count_ref, *_):
        return (jnp.minimum(i, (count_ref[0] - 1) // GROUP), 0, 0)

    return pl.pallas_call(
        functools.partial(product_kernel, len(sources), len(out_rows), transpose),
        grid_spec=pltpu.PrefetchScalarGridSpec(
            num_scalar_prefetch=3,
            grid=(values.shape[0] // GROUP,),
            in_specs=[pl.BlockSpec((GROUP, TILE, TILE), tile_at)]
            + [pl.BlockSpec((s.shape[0], width), lambda i, *_: (0, chunk)) for s in sources],
            out_specs=[pl.BlockSpec((r, width), lambda i, *_: (0, 0)) for r in out_rows],
            scratch_shapes=[pltpu.VMEM((rows, width), BF), pltpu.VMEM((sum(out_rows), width), F32)],
        ),
        out_shape=[jax.ShapeDtypeStruct((r, width), BF) for r in out_rows],
        compiler_params=pltpu.CompilerParams(vmem_limit_bytes=58 * 2**20),
        cost_estimate=pl.CostEstimate(
            flops=2 * values.shape[0] * TILE * TILE * width,
            bytes_accessed=2 * values.size + 2 * (rows + sum(out_rows)) * width,
            transcendentals=0,
        ),
    )(count, src_idx, dst_idx, values, *sources)


def from_z(x, s):
    return lax.ppermute(x, "row", [(i, (i & 4) | ((i - s) & 3)) for i in range(8)])


def from_y(x, s):
    return lax.ppermute(x, "col", [(i, (i - 4 * s) & 15) for i in range(16)])


def swap(x, axis, bit):
    return lax.ppermute(x, axis, [(i, i ^ bit) for i in range(lax.axis_size(axis))])


def gather(x, far, axis, bit):
    other = swap(x, axis, bit)
    pieces = [x, other]
    for s in (1, 2, 3):
        pieces += [far(x, s), far(other, s)]
    return pieces


def send_pieces(parts, far):
    return {s: far(parts[s].astype(BF), -s) for s in (1, 3, 2)}


def add_pieces(own, got, axis, bit):
    total = own.astype(F32) + sum(g.astype(F32) for g in got.values())
    rows = total.shape[0] // 2
    across = swap(total[rows:].astype(BF), axis, bit)
    return total[:rows] + across.astype(F32)


def all_sum(x, extra, got):
    col, row = lax.axis_index("col"), lax.axis_index("row")
    path = []
    for bit, axis, at in ((1, "col", col), (2, "col", col)):
        half = x.shape[0] // 2
        side = (at // bit) & 1
        mine = lax.dynamic_slice_in_dim(x, side * half, half, 0)
        theirs = lax.dynamic_slice_in_dim(x, (1 - side) * half, half, 0)
        x = mine + swap(theirs.astype(BF), axis, bit).astype(F32)
        path.append((side, axis, bit))
    x, got[1], got[3] = lax.optimization_barrier((x, got[1], got[3]))
    quarter = x.shape[0] // 4
    y = col // 4
    own = lax.dynamic_slice_in_dim(x, y * quarter, quarter, 0)
    for s in (1, 2, 3):
        part = lax.dynamic_slice_in_dim(x, ((y + s) & 3) * quarter, quarter, 0)
        own = own + from_y(part.astype(BF), -s).astype(F32)
    own = jnp.concatenate([own, jnp.broadcast_to(extra[None], (8, extra.shape[0]))], 0)
    own = own + swap(own, "row", 4)
    far = [from_z(own, s) for s in (1, 2, 3)]
    own = own + far[0] + far[1] + far[2]
    extra = own[-1]
    x = own[:-8].astype(BF)
    pieces = jnp.stack([x] + [from_y(x, s) for s in (1, 2, 3)])
    x = jnp.concatenate([lax.dynamic_index_in_dim(pieces, (k - y) & 3, 0, False) for k in range(4)], 0)
    for side, axis, bit in reversed(path):
        other = swap(x, axis, bit)
        low = jnp.where(side == 0, x, other)
        high = jnp.where(side == 0, other, x)
        x = jnp.concatenate([low, high], 0)
    return x.astype(F32), extra


def body(features, weight, bias, cotangent, tile_values, tile_row, tile_col, tile_count):
    width = weight.shape[1] // CHUNKS
    row, col = lax.axis_index("row"), lax.axis_index("col")
    dest = tile_row[0] >> 2
    order = ((dest ^ col) & 1) * 8 + (((dest >> 2) - (col >> 2)) & 3) * 2 + (((dest ^ col) >> 1) & 1)
    row_idx = order * 4 + (tile_row[0] & 3)
    owner = tile_col[0] >> 2
    order = ((owner - row) & 3) * 2 + (((owner ^ row) >> 2) & 1)
    col_idx = order * 4 + (tile_col[0] & 3)

    feats = gather(features, from_z, "row", 4)
    hidden = [jnp.dot(f, weight, preferred_element_type=F32).astype(BF) for f in feats]

    outputs, features_sum, weight_terms, bias_sums = [], None, [], []
    for chunk in range(CHUNKS):
        cols = slice(chunk * width, (chunk + 1) * width)
        mine, theirs = product(
            tile_values, tile_count, col_idx, row_idx, hidden, chunk, width, [8 * SPAN] * 2, False
        )
        theirs = swap(theirs, "col", 1)
        both = mine.astype(F32) + theirs.astype(F32)
        parts = [both[s * 2 * SPAN : (s + 1) * 2 * SPAN] for s in range(4)]
        got = send_pieces(parts, from_y)
        summed_input = add_pieces(parts[0], got, "col", 2) + bias[None, cols]
        sigma = jax.nn.sigmoid(summed_input)
        outputs.append((summed_input * sigma).astype(BF))
        grad_own = (
            cotangent[:, cols].astype(F32) * sigma * (1.0 + summed_input * (1.0 - sigma))
        ).astype(BF)
        grads = gather(grad_own, from_y, "col", 2)
        grads = grads + [swap(g, "col", 1) for g in grads]
        bias_sum = sum(jnp.sum(g.astype(F32), axis=0) for g in grads)
        backs = product(
            tile_values, tile_count, row_idx, col_idx, grads, 0, width, [2 * SPAN] * 4, True
        )
        got = send_pieces(backs, from_z)
        term = sum(
            lax.dot_general(
                feats[2 * s + t],
                backs[s][t * SPAN : (t + 1) * SPAN],
                (((0,), (0,)), ((), ())),
                preferred_element_type=F32,
            )
            for s in range(4)
            for t in range(2)
        )
        term, bias_sum = all_sum(term, bias_sum, got)
        weight_terms.append(term)
        bias_sums.append(bias_sum)
        back_own = add_pieces(backs[0], got, "row", 4)
        term = lax.dot_general(
            back_own.astype(BF), weight[:, cols], (((1,), (1,)), ((), ())), preferred_element_type=F32
        )
        features_sum = term if features_sum is None else features_sum + term
    return (
        jnp.concatenate(outputs, 1),
        features_sum.astype(BF),
        jnp.concatenate(weight_terms, 1),
        jnp.concatenate(bias_sums),
    )


def solution(mesh):
    in_specs = (
        P(("row", "col"), None),
        P(),
        P(),
        P(("row", "col"), None),
        P(("row", "col"), None, None),
        P(("row", "col"), None),
        P(("row", "col"), None),
        P(("row", "col")),
    )
    out_specs = (P(("row", "col"), None), P(("row", "col"), None), P(), P())
    return jax.shard_map(body, mesh=mesh, in_specs=in_specs, out_specs=out_specs, check_vma=False)
```

```python
import functools

import jax
import jax.numpy as jnp
from jax import lax
from jax.experimental import pallas as pl
from jax.experimental.pallas import tpu as pltpu
from jax.sharding import PartitionSpec as P

GROUP = 16
TILE = 128
BF = jnp.bfloat16
F32 = jnp.float32


def product_kernel(n_src, n_out, transpose, count_ref, src_idx, dst_idx, values, *refs):
    sources, outs = refs[:n_src], refs[n_src : n_src + n_out]
    source, total = refs[n_src + n_out :]
    step = pl.program_id(0)

    @pl.when(step == 0)
    def _():
        at = 0
        for ref in sources:
            source[at : at + ref.shape[0], :] = ref[...]
            at += ref.shape[0]
        source[at:, :] = jnp.zeros((TILE, source.shape[1]), BF)
        total[...] = jnp.zeros_like(total)

    def one(t):
        slot = step * GROUP + t
        start = pl.multiple_of(src_idx[slot] * TILE, TILE)
        end = pl.multiple_of(dst_idx[slot] * TILE, TILE)
        block = source[pl.ds(start, TILE), :]
        dims = (((0,), (0,)), ((), ())) if transpose else (((1,), (0,)), ((), ()))
        total[pl.ds(end, TILE), :] += lax.dot_general(
            values[t], block, dims, preferred_element_type=F32
        )

    @pl.when(step * GROUP < count_ref[0])
    def _():
        for t in range(GROUP):
            one(t)

    @pl.when(step == pl.num_programs(0) - 1)
    def _():
        at = 0
        for ref in outs:
            ref[...] = total[at : at + ref.shape[0], :].astype(BF)
            at += ref.shape[0]


def product(values, count, src_idx, dst_idx, sources, chunk, width, out_rows, transpose):
    rows = sum(s.shape[0] for s in sources)
    used = jnp.arange(values.shape[0], dtype=jnp.int32) < count
    src_idx = jnp.where(used, src_idx, rows // TILE)

    def tile_at(i, count_ref, *_):
        return (jnp.minimum(i, (count_ref[0] - 1) // GROUP), 0, 0)

    return pl.pallas_call(
        functools.partial(product_kernel, len(sources), len(out_rows), transpose),
        grid_spec=pltpu.PrefetchScalarGridSpec(
            num_scalar_prefetch=3,
            grid=(values.shape[0] // GROUP,),
            in_specs=[pl.BlockSpec((GROUP, TILE, TILE), tile_at)]
            + [pl.BlockSpec((s.shape[0], width), lambda i, *_: (0, chunk)) for s in sources],
            out_specs=[pl.BlockSpec((r, width), lambda i, *_: (0, 0)) for r in out_rows],
            scratch_shapes=[pltpu.VMEM((rows + TILE, width), BF), pltpu.VMEM((sum(out_rows), width), F32)],
        ),
        out_shape=[jax.ShapeDtypeStruct((r, width), BF) for r in out_rows],
        compiler_params=pltpu.CompilerParams(vmem_limit_bytes=58 * 2**20),
        cost_estimate=pl.CostEstimate(
            flops=2 * values.shape[0] * TILE * TILE * width,
            bytes_accessed=2 * values.size + 2 * (rows + sum(out_rows)) * width,
            transcendentals=0,
        ),
    )(count, src_idx, dst_idx, values, *sources)


def from_z(x, s):
    return lax.ppermute(x, "row", [(i, (i & 4) | ((i - s) & 3)) for i in range(8)])


def from_y(x, s):
    return lax.ppermute(x, "col", [(i, (i - 4 * s) & 15) for i in range(16)])


def swap(x, axis, bit):
    return lax.ppermute(x, axis, [(i, i ^ bit) for i in range(lax.axis_size(axis))])


def gather_across_first(x, far, axis, bit):
    other = swap(x, axis, bit)
    pieces = [x, other]
    for s in (1, 2, 3):
        pieces += [far(x, s), far(other, s)]
    return pieces


def gather_along_first(x, far, axis, bit, pieces):
    near = jnp.concatenate([x] + [far(x, s) for s in (1, 2, 3)], 0)
    near, pieces[1] = lax.optimization_barrier((near, pieces[1]))
    return [near, swap(near, axis, bit)]


def send_along(parts, far):
    return {s: far(parts[s].astype(BF), -s) for s in (1, 3, 2)}


def end_across(own, got, axis, bit):
    total = own.astype(F32) + sum(g.astype(F32) for g in got.values())
    rows = total.shape[0] // 2
    across = swap(total[rows:].astype(BF), axis, bit)
    return total[:rows] + across.astype(F32)


def end_along(own, across, far):
    total = own.astype(F32) + across.astype(F32)
    rows = total.shape[0] // 4
    parts = [total[s * rows : (s + 1) * rows] for s in range(4)]
    return parts[0] + sum(g.astype(F32) for g in send_along(parts, far).values())


def with_rows(x, extra):
    return jnp.concatenate([x, jnp.broadcast_to(extra[None], (16, extra.shape[0]))], 0).astype(BF)


def halve(x, extra, axis, bit):
    half = x.shape[0] // 2
    side = (lax.axis_index(axis) // bit) & 1
    mine = lax.dynamic_slice_in_dim(x, side * half, half, 0)
    theirs = lax.dynamic_slice_in_dim(x, (1 - side) * half, half, 0)
    got = swap(with_rows(theirs, extra), axis, bit).astype(F32)
    return mine + got[:half], extra + got[half]


def join(x, axis, bit):
    side = (lax.axis_index(axis) // bit) & 1
    x = x.astype(BF)
    other = swap(x, axis, bit)
    return jnp.concatenate([jnp.where(side == 0, x, other), jnp.where(side == 0, other, x)], 0)


def add_all(x, extra, far):
    rows = x.shape[0]
    sent = with_rows(x, extra)
    got = sum(far(sent, s).astype(F32) for s in (1, 2, 3)) + sent.astype(F32)
    return got[:rows], got[rows]


def place(block, side, along, across, sides):
    half, part = (block >> 1) & 1, block & 1
    order = jnp.where(half == 0, along * 2 + across, across * 4 + along)
    return ((half * sides + side) * 8 + order) * 2 + part


def body(features, weight, bias, cotangent, tile_values, tile_row, tile_col, tile_count):
    width = weight.shape[1]
    half = features.shape[0] // 2
    row, col = lax.axis_index("row"), lax.axis_index("col")
    dest = tile_row[0] >> 2
    row_idx = place(
        tile_row[0], (dest ^ col) & 1, ((dest >> 2) - (col >> 2)) & 3, ((dest ^ col) >> 1) & 1, 2
    )
    owner = tile_col[0] >> 2
    col_idx = place(tile_col[0], 0, (owner - row) & 3, ((owner ^ row) >> 2) & 1, 1)

    feats = gather_across_first(features[:half], from_z, "row", 4)
    feats += gather_along_first(features[half:], from_z, "row", 4, feats)

    mine_0, theirs_0, mine_1, theirs_1 = product(
        tile_values, tile_count, col_idx, row_idx, feats, 0, width, [8 * half] * 4, False
    )
    theirs_1 = swap(theirs_1, "col", 1)
    theirs_0 = swap(theirs_0, "col", 1)
    far_1 = mine_1[4 * half :].astype(F32) + theirs_1[4 * half :].astype(F32)
    far_1 = swap(far_1.astype(BF), "col", 2)
    both = mine_0.astype(F32) + theirs_0.astype(F32)
    parts = [both[s * 2 * half : (s + 1) * 2 * half] for s in range(4)]
    got = send_along(parts, from_y)
    sum_1 = end_along(
        mine_1[: 4 * half].astype(F32) + theirs_1[: 4 * half].astype(F32), far_1, from_y
    )
    sum_0 = end_across(parts[0], got, "col", 2)

    def activation(total, rows):
        summed = total.astype(BF)
        summed_input = jnp.dot(summed, weight, preferred_element_type=F32) + bias[None, :]
        sigma = jax.nn.sigmoid(summed_input)
        output = (summed_input * sigma).astype(BF)
        grad = cotangent[rows].astype(F32) * sigma * (1.0 + summed_input * (1.0 - sigma))
        return summed, output, grad.astype(BF)

    summed_0, output_0, grad_0 = activation(sum_0, slice(0, half))
    pieces = gather_across_first(grad_0, from_y, "col", 2)
    summed_1, output_1, grad_1 = activation(sum_1, slice(half, 2 * half))
    other = gather_along_first(grad_1, from_y, "col", 2, pieces)
    grads = [jnp.concatenate(pieces[:4], 0), jnp.concatenate(pieces[4:], 0)]
    grads += [swap(p, "col", 1) for p in grads]
    grads += other + [swap(p, "col", 1) for p in other]

    grad_weight = sum(
        lax.dot_general(s, g, (((0,), (0,)), ((), ())), preferred_element_type=F32)
        for s, g in ((summed_0, grad_0), (summed_1, grad_1))
    )
    grad_bias = jnp.sum(grad_0.astype(F32), axis=0) + jnp.sum(grad_1.astype(F32), axis=0)
    grad_weight, grad_bias = halve(grad_weight, grad_bias, "row", 4)
    grad_weight, grad_bias = add_all(grad_weight, grad_bias, from_z)
    grads[0], grad_weight = lax.optimization_barrier((grads[0], grad_weight))
    grad_weight = join(grad_weight, "row", 4)

    *backs, near_1, far_1 = product(
        tile_values, tile_count, row_idx, col_idx, grads, 0, width, [2 * half] * 4 + [4 * half] * 2, True
    )
    got = send_along(backs, from_z)
    far_1 = swap(far_1, "row", 4)
    for bit in (1, 2):
        grad_weight, grad_bias = halve(grad_weight, grad_bias, "col", bit)
    grad_weight, got[1], got[3] = lax.optimization_barrier((grad_weight, got[1], got[3]))
    grad_weight, grad_bias = add_all(grad_weight, grad_bias, from_y)
    for bit in (2, 1):
        grad_weight = join(grad_weight, "col", bit)
    back_1 = end_along(near_1, far_1, from_z)
    back_0 = end_across(backs[0], got, "row", 4)
    grad_features = [
        lax.dot_general(
            b.astype(BF), weight, (((1,), (1,)), ((), ())), preferred_element_type=F32
        ).astype(BF)
        for b in (back_0, back_1)
    ]
    return (
        jnp.concatenate([output_0, output_1], 0),
        jnp.concatenate(grad_features, 0),
        grad_weight.astype(F32),
        grad_bias,
    )


def solution(mesh):
    in_specs = (
        P(("row", "col"), None),
        P(),
        P(),
        P(("row", "col"), None),
        P(("row", "col"), None, None),
        P(("row", "col"), None),
        P(("row", "col"), None),
        P(("row", "col")),
    )
    out_specs = (P(("row", "col"), None), P(("row", "col"), None), P(), P())
    return jax.shard_map(body, mesh=mesh, in_specs=in_specs, out_specs=out_specs, check_vma=False)
```

```python
import functools

import jax
import jax.numpy as jnp
from jax import lax
from jax.experimental import pallas as pl
from jax.experimental.pallas import tpu as pltpu
from jax.sharding import PartitionSpec as P

GROUP = 32
TILE = 128
BF = jnp.bfloat16
F32 = jnp.float32


def product_kernel(n_src, n_out, transpose, count_ref, src_idx, dst_idx, values, *refs):
    sources, outs = refs[:n_src], refs[n_src : n_src + n_out]
    tiles, source, total, staged, sem_source, sem_tile, sem_out = refs[n_src + n_out :]
    groups = (count_ref[0] + GROUP - 1) // GROUP
    arriving = []
    at = 0
    for k, ref in enumerate(sources):
        here = source.at[pl.ds(at, ref.shape[0]), :]
        arriving.append(pltpu.make_async_copy(ref, here, sem_source.at[k]))
        at += ref.shape[0]
    for copy in arriving:
        copy.start()

    def tile_copy(g):
        part = pl.ds(g * GROUP, GROUP)
        return pltpu.make_async_copy(values.at[part], tiles.at[part], sem_tile.at[g])

    @pl.loop(0, groups)
    def _(g):
        tile_copy(g).start()

    source[at:, :] = jnp.zeros((TILE, source.shape[1]), BF)
    total[...] = jnp.zeros_like(total)
    for copy in arriving:
        copy.wait()

    def one(slot):
        start = pl.multiple_of(src_idx[slot] * TILE, TILE)
        end = pl.multiple_of(dst_idx[slot] * TILE, TILE)
        block = source[pl.ds(start, TILE), :]
        dims = (((0,), (0,)), ((), ())) if transpose else (((1,), (0,)), ((), ()))
        total[pl.ds(end, TILE), :] += lax.dot_general(
            tiles[slot], block, dims, preferred_element_type=F32
        )

    @pl.loop(0, groups)
    def _(g):
        tile_copy(g).wait()
        for t in range(GROUP):
            one(g * GROUP + t)

    leaving = []
    at = 0
    for k, ref in enumerate(outs):
        part = pl.ds(at, ref.shape[0])
        staged[part, :] = total[part, :].astype(BF)
        leaving.append(pltpu.make_async_copy(staged.at[part, :], ref, sem_out.at[k]))
        leaving[-1].start()
        at += ref.shape[0]
    for copy in leaving:
        copy.wait()


def product(values, count, src_idx, dst_idx, sources, out_rows, transpose):
    rows, width = sum(s.shape[0] for s in sources), sources[0].shape[1]
    slots = values.shape[0]
    used = jnp.arange(slots, dtype=jnp.int32) < count
    src_idx = jnp.where(used, src_idx, rows // TILE)
    anywhere = pl.BlockSpec(memory_space=pl.ANY)
    return pl.pallas_call(
        functools.partial(product_kernel, len(sources), len(out_rows), transpose),
        in_specs=[pl.BlockSpec(memory_space=pltpu.SMEM)] * 3 + [anywhere] * (1 + len(sources)),
        out_specs=[anywhere] * len(out_rows),
        scratch_shapes=[
            pltpu.VMEM(values.shape, BF),
            pltpu.VMEM((rows + TILE, width), BF),
            pltpu.VMEM((sum(out_rows), width), F32),
            pltpu.VMEM((sum(out_rows), width), BF),
            pltpu.SemaphoreType.DMA((len(sources),)),
            pltpu.SemaphoreType.DMA((slots // GROUP,)),
            pltpu.SemaphoreType.DMA((len(out_rows),)),
        ],
        out_shape=[jax.ShapeDtypeStruct((r, width), BF) for r in out_rows],
        compiler_params=pltpu.CompilerParams(vmem_limit_bytes=60 * 2**20),
        cost_estimate=pl.CostEstimate(
            flops=2 * slots * TILE * TILE * width,
            bytes_accessed=2 * values.size + 2 * (rows + sum(out_rows)) * width,
            transcendentals=0,
        ),
    )(count, src_idx, dst_idx, values, *sources)


def from_z(x, s):
    return lax.ppermute(x, "row", [(i, (i & 4) | ((i - s) & 3)) for i in range(8)])


def from_y(x, s):
    return lax.ppermute(x, "col", [(i, (i - 4 * s) & 15) for i in range(16)])


def swap(x, axis, bit):
    return lax.ppermute(x, axis, [(i, i ^ bit) for i in range(lax.axis_size(axis))])


def gather_across_first(x, far, axis, bit):
    near = jnp.concatenate([x, swap(x, axis, bit)], 0)
    return [near] + [far(near, s) for s in (1, 2, 3)]


def gather_along(x, far):
    return jnp.concatenate([x] + [far(x, s) for s in (1, 2, 3)], 0)


def send_along(parts, far):
    return {s: far(parts[s].astype(BF), -s) for s in (1, 3, 2)}


def end_across(own, got, axis, bit):
    total = own.astype(F32) + sum(g.astype(F32) for g in got.values())
    rows = total.shape[0] // 2
    across = swap(total[rows:].astype(BF), axis, bit)
    return total[:rows] + across.astype(F32)


def meet_across(own, across):
    total = own.astype(F32) + across.astype(F32)
    rows = total.shape[0] // 4
    return [total[s * rows : (s + 1) * rows] for s in range(4)]


def end_along(own, got):
    return own + sum(g.astype(F32) for g in got.values())


def with_rows(x, extra):
    return jnp.concatenate([x, jnp.broadcast_to(extra[None], (16, extra.shape[0]))], 0).astype(BF)


def halve(x, extra, axis, bit):
    half = x.shape[0] // 2
    side = (lax.axis_index(axis) // bit) & 1
    mine = lax.dynamic_slice_in_dim(x, side * half, half, 0)
    theirs = lax.dynamic_slice_in_dim(x, (1 - side) * half, half, 0)
    got = swap(with_rows(theirs, extra), axis, bit).astype(F32)
    return mine + got[:half], extra.astype(BF).astype(F32) + got[half]


def join(x, axis, bit):
    side = (lax.axis_index(axis) // bit) & 1
    x = x.astype(BF)
    other = swap(x, axis, bit)
    return jnp.concatenate([jnp.where(side == 0, x, other), jnp.where(side == 0, other, x)], 0)


def add_all(x, extra, far):
    rows = x.shape[0]
    sent = with_rows(x, extra)
    got = {s: far(sent, s).astype(F32) for s in (1, 2, 3)}
    total = (sent.astype(F32) + got[2]) + (got[1] + got[3])
    return total[:rows], total[rows]


def add_pair(x, extra, axis, bit):
    rows = x.shape[0]
    sent = with_rows(x, extra)
    total = sent.astype(F32) + swap(sent, axis, bit).astype(F32)
    return total[:rows], total[rows]


def place(block, side, along, across, sides):
    half, part = (block >> 1) & 1, block & 1
    order = jnp.where(half == 0, along * 2 + across, across * 4 + along)
    return ((half * sides + side) * 8 + order) * 2 + part


def body(features, weight, bias, cotangent, tile_values, tile_row, tile_col, tile_count):
    half = features.shape[0] // 2
    row, col = lax.axis_index("row"), lax.axis_index("col")
    dest = tile_row[0] >> 2
    row_idx = place(
        tile_row[0], (dest ^ col) & 1, ((dest >> 2) - (col >> 2)) & 3, ((dest ^ col) >> 1) & 1, 2
    )
    owner = tile_col[0] >> 2
    col_idx = place(tile_col[0], 0, (owner - row) & 3, ((owner ^ row) >> 2) & 1, 1)

    feats = gather_across_first(features[:half], from_z, "row", 4)
    near = gather_along(features[half:], from_z)
    near, feats[0] = lax.optimization_barrier((near, feats[0]))
    feats += [near, swap(near, "row", 4)]

    mine_0, theirs_0, mine_1, theirs_1 = product(
        tile_values, tile_count, col_idx, row_idx, feats, [8 * half] * 4, False
    )
    theirs_1 = swap(theirs_1, "col", 1)
    theirs_0 = swap(theirs_0, "col", 1)
    far_1 = mine_1[4 * half :].astype(F32) + theirs_1[4 * half :].astype(F32)
    far_1 = swap(far_1.astype(BF), "col", 2)
    both = mine_0.astype(F32) + theirs_0.astype(F32)
    parts = [both[s * 2 * half : (s + 1) * 2 * half] for s in range(4)]
    got = send_along(parts, from_y)
    parts_1 = meet_across(mine_1[: 4 * half].astype(F32) + theirs_1[: 4 * half].astype(F32), far_1)
    got_1 = send_along(parts_1, from_y)
    got[2], got_1[1] = lax.optimization_barrier((got[2], got_1[1]))
    sum_1 = end_along(parts_1[0], got_1)
    sum_0 = end_across(parts[0], got, "col", 2)

    def activation(total, rows):
        summed = total.astype(BF)
        summed_input = jnp.dot(summed, weight, preferred_element_type=F32) + bias[None, :]
        sigma = jax.nn.sigmoid(summed_input)
        output = (summed_input * sigma).astype(BF)
        grad = cotangent[rows].astype(F32) * sigma * (1.0 + summed_input * (1.0 - sigma))
        return summed, output, grad.astype(BF)

    summed_0, output_0, grad_0 = activation(sum_0, slice(0, half))
    pieces = gather_across_first(grad_0, from_y, "col", 2)
    summed_1, output_1, grad_1 = activation(sum_1, slice(half, 2 * half))
    near = gather_along(grad_1, from_y)

    grad_0, grad_1 = lax.optimization_barrier((grad_0, grad_1))
    grad_weight = sum(
        lax.dot_general(s, g, (((0,), (0,)), ((), ())), preferred_element_type=F32)
        for s, g in ((summed_0, grad_0), (summed_1, grad_1))
    )
    grad_bias = jnp.sum(grad_0.astype(F32), axis=0) + jnp.sum(grad_1.astype(F32), axis=0)
    grad_weight, grad_bias = halve(grad_weight, grad_bias, "col", 1)
    grad_weight, grad_bias = halve(grad_weight, grad_bias, "row", 4)

    near, grad_weight, pieces[0] = lax.optimization_barrier((near, grad_weight, pieces[0]))
    other = [near, swap(near, "col", 2)]
    grad_weight, other[1] = lax.optimization_barrier((grad_weight, other[1]))
    grad_weight, grad_bias = add_all(grad_weight, grad_bias, from_z)
    grads = pieces + [swap(p, "col", 1) for p in pieces]
    grads += other + [swap(p, "col", 1) for p in other]
    grads[0], grad_weight = lax.optimization_barrier((grads[0], grad_weight))

    *backs, near_1, far_1 = product(
        tile_values, tile_count, row_idx, col_idx, grads, [2 * half] * 4 + [4 * half] * 2, True
    )
    got = send_along(backs, from_z)
    far_1 = swap(far_1, "row", 4)
    grad_weight, got[1] = lax.optimization_barrier((grad_weight, got[1]))
    grad_weight, grad_bias = add_all(grad_weight, grad_bias, from_y)
    grad_weight, grad_bias = add_pair(grad_weight, grad_bias, "col", 2)
    grad_weight, far_1 = lax.optimization_barrier((grad_weight, far_1))
    parts_1 = meet_across(near_1, far_1)
    got_1 = send_along(parts_1, from_z)
    grad_weight = join(grad_weight, "row", 4)
    grad_weight, got_1[1], got_1[3] = lax.optimization_barrier((grad_weight, got_1[1], got_1[3]))
    grad_weight = join(grad_weight, "col", 1)
    back_1 = end_along(parts_1[0], got_1)
    back_0 = end_across(backs[0], got, "row", 4)
    grad_features = [
        lax.dot_general(
            b.astype(BF), weight, (((1,), (1,)), ((), ())), preferred_element_type=F32
        ).astype(BF)
        for b in (back_0, back_1)
    ]
    return (
        jnp.concatenate([output_0, output_1], 0),
        jnp.concatenate(grad_features, 0),
        grad_weight.astype(F32),
        grad_bias,
    )


def solution(mesh):
    in_specs = (
        P(("row", "col"), None),
        P(),
        P(),
        P(("row", "col"), None),
        P(("row", "col"), None, None),
        P(("row", "col"), None),
        P(("row", "col"), None),
        P(("row", "col")),
    )
    out_specs = (P(("row", "col"), None), P(("row", "col"), None), P(), P())
    return jax.shard_map(body, mesh=mesh, in_specs=in_specs, out_specs=out_specs, check_vma=False)
```

```python
import functools

import jax
import jax.numpy as jnp
from jax import lax
from jax.experimental import pallas as pl
from jax.experimental.pallas import tpu as pltpu
from jax.sharding import PartitionSpec as P

GROUP = 32
TILE = 128
BF = jnp.bfloat16
F32 = jnp.float32


def product_kernel(n_src, n_out, transpose, count_ref, src_idx, dst_idx, values, *refs):
    sources, outs = refs[:n_src], refs[n_src : n_src + n_out]
    tiles, source, total, staged, sem_source, sem_tile, sem_out = refs[n_src + n_out :]
    groups = (count_ref[0] + GROUP - 1) // GROUP
    arriving = []
    at = 0
    for k, ref in enumerate(sources):
        here = source.at[pl.ds(at, ref.shape[0]), :]
        arriving.append(pltpu.make_async_copy(ref, here, sem_source.at[k]))
        at += ref.shape[0]
    for copy in arriving:
        copy.start()

    def tile_copy(g):
        part = pl.ds(g * GROUP, GROUP)
        return pltpu.make_async_copy(values.at[part], tiles.at[part], sem_tile.at[g])

    @pl.loop(0, groups)
    def _(g):
        tile_copy(g).start()

    source[at:, :] = jnp.zeros((TILE, source.shape[1]), BF)
    total[...] = jnp.zeros_like(total)
    for copy in arriving:
        copy.wait()

    def one(slot):
        start = pl.multiple_of(src_idx[slot] * TILE, TILE)
        end = pl.multiple_of(dst_idx[slot] * TILE, TILE)
        block = source[pl.ds(start, TILE), :]
        dims = (((0,), (0,)), ((), ())) if transpose else (((1,), (0,)), ((), ()))
        total[pl.ds(end, TILE), :] += lax.dot_general(
            tiles[slot], block, dims, preferred_element_type=F32
        )

    @pl.loop(0, groups)
    def _(g):
        tile_copy(g).wait()
        for t in range(GROUP):
            one(g * GROUP + t)

    leaving = []
    at = 0
    for k, ref in enumerate(outs):
        part = pl.ds(at, ref.shape[0])
        staged[part, :] = total[part, :].astype(BF)
        leaving.append(pltpu.make_async_copy(staged.at[part, :], ref, sem_out.at[k]))
        leaving[-1].start()
        at += ref.shape[0]
    for copy in leaving:
        copy.wait()


def product(values, count, src_idx, dst_idx, sources, out_rows, transpose):
    rows, width = sum(s.shape[0] for s in sources), sources[0].shape[1]
    slots = values.shape[0]
    used = jnp.arange(slots, dtype=jnp.int32) < count
    src_idx = jnp.where(used, src_idx, rows // TILE)
    anywhere = pl.BlockSpec(memory_space=pl.ANY)
    return pl.pallas_call(
        functools.partial(product_kernel, len(sources), len(out_rows), transpose),
        in_specs=[pl.BlockSpec(memory_space=pltpu.SMEM)] * 3 + [anywhere] * (1 + len(sources)),
        out_specs=[anywhere] * len(out_rows),
        scratch_shapes=[
            pltpu.VMEM(values.shape, BF),
            pltpu.VMEM((rows + TILE, width), BF),
            pltpu.VMEM((sum(out_rows), width), F32),
            pltpu.VMEM((sum(out_rows), width), BF),
            pltpu.SemaphoreType.DMA((len(sources),)),
            pltpu.SemaphoreType.DMA((slots // GROUP,)),
            pltpu.SemaphoreType.DMA((len(out_rows),)),
        ],
        out_shape=[jax.ShapeDtypeStruct((r, width), BF) for r in out_rows],
        compiler_params=pltpu.CompilerParams(vmem_limit_bytes=60 * 2**20),
        cost_estimate=pl.CostEstimate(
            flops=2 * slots * TILE * TILE * width,
            bytes_accessed=2 * values.size + 2 * (rows + sum(out_rows)) * width,
            transcendentals=0,
        ),
    )(count, src_idx, dst_idx, values, *sources)


def from_z(x, s):
    return lax.ppermute(x, "row", [(i, (i & 4) | ((i - s) & 3)) for i in range(8)])


def from_y(x, s):
    return lax.ppermute(x, "col", [(i, (i - 4 * s) & 15) for i in range(16)])


def swap(x, axis, bit):
    return lax.ppermute(x, axis, [(i, i ^ bit) for i in range(lax.axis_size(axis))])


def gather_across_first(x, far, axis, bit):
    near = jnp.concatenate([x, swap(x, axis, bit)], 0)
    return [near] + [far(near, s) for s in (1, 2, 3)]


def gather_along(x, far):
    return jnp.concatenate([x] + [far(x, s) for s in (1, 2, 3)], 0)


def send_along(parts, far):
    return {s: far(parts[s].astype(BF), -s) for s in (1, 3, 2)}


def end_across(own, got, axis, bit):
    total = own.astype(F32) + sum(g.astype(F32) for g in got.values())
    rows = total.shape[0] // 2
    across = swap(total[rows:].astype(BF), axis, bit)
    return total[:rows] + across.astype(F32)


def meet_across(own, across):
    total = own.astype(F32) + across.astype(F32)
    rows = total.shape[0] // 4
    return [total[s * rows : (s + 1) * rows] for s in range(4)]


def end_along(own, got):
    return own + sum(g.astype(F32) for g in got.values())


def with_rows(x, extra):
    return jnp.concatenate([x, jnp.broadcast_to(extra[None], (16, extra.shape[0]))], 0).astype(BF)


def halve(x, extra, axis, bit):
    half = x.shape[0] // 2
    side = (lax.axis_index(axis) // bit) & 1
    mine = lax.dynamic_slice_in_dim(x, side * half, half, 0)
    theirs = lax.dynamic_slice_in_dim(x, (1 - side) * half, half, 0)
    got = swap(with_rows(theirs, extra), axis, bit).astype(F32)
    return mine + got[:half], extra.astype(BF).astype(F32) + got[half]


def join(x, axis, bit):
    side = (lax.axis_index(axis) // bit) & 1
    x = x.astype(BF)
    other = swap(x, axis, bit)
    return jnp.concatenate([jnp.where(side == 0, x, other), jnp.where(side == 0, other, x)], 0)


def add_all(x, extra, far):
    rows = x.shape[0]
    sent = with_rows(x, extra)
    got = {s: far(sent, s).astype(F32) for s in (1, 2, 3)}
    total = (sent.astype(F32) + got[2]) + (got[1] + got[3])
    return total[:rows], total[rows]


def add_pair(x, extra, axis, bit):
    rows = x.shape[0]
    sent = with_rows(x, extra)
    total = sent.astype(F32) + swap(sent, axis, bit).astype(F32)
    return total[:rows], total[rows]


def place(block, side, along, across, sides):
    half, part = (block >> 1) & 1, block & 1
    order = jnp.where(half == 0, along * 2 + across, across * 4 + along)
    return ((half * sides + side) * 8 + order) * 2 + part


def body(features, weight, bias, cotangent, tile_values, tile_row, tile_col, tile_count):
    half = features.shape[0] // 2
    row, col = lax.axis_index("row"), lax.axis_index("col")
    dest = tile_row[0] >> 2
    row_idx = place(
        tile_row[0], (dest ^ col) & 1, ((dest >> 2) - (col >> 2)) & 3, ((dest ^ col) >> 1) & 1, 2
    )
    owner = tile_col[0] >> 2
    col_idx = place(tile_col[0], 0, (owner - row) & 3, ((owner ^ row) >> 2) & 1, 1)

    feats = gather_across_first(features[:half], from_z, "row", 4)
    near = gather_along(features[half:], from_z)
    near, feats[0] = lax.optimization_barrier((near, feats[0]))
    feats += [near, swap(near, "row", 4)]

    mine_0, theirs_0, mine_1, theirs_1 = product(
        tile_values, tile_count, col_idx, row_idx, feats, [8 * half] * 4, False
    )
    theirs_1 = swap(theirs_1, "col", 1)
    theirs_0 = swap(theirs_0, "col", 1)
    far_1 = mine_1[4 * half :].astype(F32) + theirs_1[4 * half :].astype(F32)
    far_1 = swap(far_1.astype(BF), "col", 2)
    both = mine_0.astype(F32) + theirs_0.astype(F32)
    parts = [both[s * 2 * half : (s + 1) * 2 * half] for s in range(4)]
    got = send_along(parts, from_y)
    parts_1 = meet_across(mine_1[: 4 * half].astype(F32) + theirs_1[: 4 * half].astype(F32), far_1)
    got_1 = send_along(parts_1, from_y)
    got[2], got_1[1] = lax.optimization_barrier((got[2], got_1[1]))
    sum_1 = end_along(parts_1[0], got_1)
    sum_0 = end_across(parts[0], got, "col", 2)

    def activation(total, rows):
        summed = total.astype(BF)
        summed_input = jnp.dot(summed, weight, preferred_element_type=F32) + bias[None, :]
        sigma = jax.nn.sigmoid(summed_input)
        output = (summed_input * sigma).astype(BF)
        grad = cotangent[rows].astype(F32) * sigma * (1.0 + summed_input * (1.0 - sigma))
        return summed, output, grad.astype(BF)

    summed_0, output_0, grad_0 = activation(sum_0, slice(0, half))
    pieces = gather_across_first(grad_0, from_y, "col", 2)
    summed_1, output_1, grad_1 = activation(sum_1, slice(half, 2 * half))
    near = gather_along(grad_1, from_y)

    grad_0, grad_1 = lax.optimization_barrier((grad_0, grad_1))
    grad_weight = sum(
        lax.dot_general(s, g, (((0,), (0,)), ((), ())), preferred_element_type=F32)
        for s, g in ((summed_0, grad_0), (summed_1, grad_1))
    )
    grad_bias = jnp.sum(grad_0.astype(F32), axis=0) + jnp.sum(grad_1.astype(F32), axis=0)
    grad_weight, grad_bias = halve(grad_weight, grad_bias, "col", 1)
    grad_weight, grad_bias = halve(grad_weight, grad_bias, "row", 4)

    near, grad_weight, pieces[0] = lax.optimization_barrier((near, grad_weight, pieces[0]))
    other = [near, swap(near, "col", 2)]
    grad_weight, other[1] = lax.optimization_barrier((grad_weight, other[1]))
    grad_weight, grad_bias = add_all(grad_weight, grad_bias, from_z)
    grads = pieces + [swap(p, "col", 1) for p in pieces]
    grads += other + [swap(p, "col", 1) for p in other]
    grads[0], grad_weight = lax.optimization_barrier((grads[0], grad_weight))

    *backs, near_1, far_1 = product(
        tile_values, tile_count, row_idx, col_idx, grads, [2 * half] * 4 + [4 * half] * 2, True
    )
    got = send_along(backs, from_z)
    far_1 = swap(far_1, "row", 4)
    grad_weight, got[1], got[3] = lax.optimization_barrier((grad_weight, got[1], got[3]))
    grad_weight, grad_bias = add_all(grad_weight, grad_bias, from_y)
    grad_weight, grad_bias = add_pair(grad_weight, grad_bias, "col", 2)
    grad_weight, far_1 = lax.optimization_barrier((grad_weight, far_1))
    got[2], far_1 = lax.optimization_barrier((got[2], far_1))
    parts_1 = meet_across(near_1, far_1)
    got_1 = send_along(parts_1, from_z)
    grad_weight = join(grad_weight, "row", 4)
    grad_weight, got_1[1], got_1[3] = lax.optimization_barrier((grad_weight, got_1[1], got_1[3]))
    grad_weight = join(grad_weight, "col", 1)
    back_1 = end_along(parts_1[0], got_1)
    back_0 = end_across(backs[0], got, "row", 4)
    grad_features = [
        lax.dot_general(
            b.astype(BF), weight, (((1,), (1,)), ((), ())), preferred_element_type=F32
        ).astype(BF)
        for b in (back_0, back_1)
    ]
    return (
        jnp.concatenate([output_0, output_1], 0),
        jnp.concatenate(grad_features, 0),
        grad_weight.astype(F32),
        grad_bias,
    )


def solution(mesh):
    in_specs = (
        P(("row", "col"), None),
        P(),
        P(),
        P(("row", "col"), None),
        P(("row", "col"), None, None),
        P(("row", "col"), None),
        P(("row", "col"), None),
        P(("row", "col")),
    )
    out_specs = (P(("row", "col"), None), P(("row", "col"), None), P(), P())
    return jax.shard_map(body, mesh=mesh, in_specs=in_specs, out_specs=out_specs, check_vma=False)
```
